32 devices in a mesh: ens: 4 (over z), role: 2 (over core), gx: 4 (over y, x).
Axes of the slice: x: 2, y: 2, z: 4, core: 2. Of those that a mesh axis runs over, the one named last changes fastest.
Arguments:
- start_conc: float32 [4, 64, 256, 256], P('ens', 'gx', 'role'), may hold values from 0.1 to 4
- target: float32 [4, 64, 256, 256], P('ens', 'gx', 'role'), may hold values from -7 to 7
- log_coef: float32 [64, 256, 256], P('gx', 'role'), may hold values from -0.7 to 0
- inv_temp: float32 [64], replicated, may hold values from 1 to 1.06
- sched_start: int32 [4], P('ens'), may hold values from 0 to 60
Outputs:
- coef_grad: float32 [64, 256, 256], P('gx', 'role')
- adjoint_start: float32 [4, 64, 256, 256], P('ens', 'gx', 'role')
- final_conc: float32 [4, 64, 256, 256], P('ens', 'gx', 'role')
The draws below stay inside these ranges and needn't reach their ends.
Inputs may be any that keep to these rules, and one draw needn't show every extreme that they name: `sched_start`: the plan entry at which each member's window begins.
All inputs are finite; a program needn't handle non-finite values.
Results may differ from the reference program's by a relative error of at most 0.00002.
Values sent between devices are 32-bit elements; how exact they have to be, the bound alone decides.
A program may use at most 128 MiB of HBM per device.

```python
import math
import jax
import jax.numpy as jnp
from jax import lax

NZ = 256
STEPS = 4
SCHED = 64
ENS = 4
NX = 64
NY = 256


def draw_log_coef(key, part):
    key = jax.random.fold_in(key, 11)
    spread = jax.random.uniform(key, (NX, NY, NZ), jnp.float32)
    return -0.7 * spread


def draw_target(key, part):
    key = jax.random.fold_in(key, 13)
    shape = (ENS, NX, NY, NZ)
    return jnp.clip(2.0 * jax.random.normal(key, shape, jnp.float32), -7.0, 7.0)


def with_ends(values, key, smallest, high):
    spot = [jax.random.randint(jax.random.fold_in(key, axis), (), 0, length) for axis, length in enumerate(values.shape)]
    longest = values.shape.index(max(values.shape))
    beside = spot[:longest] + [(spot[longest] + 1) % values.shape[longest]] + spot[longest + 1:]
    return values.at[tuple(spot)].set(smallest).at[tuple(beside)].set(high)


def level_of(own_key, dims, split, smallest, largest):
    factor_of, own = 1.0, jax.random.fold_in(own_key, 6)
    for position, shards_of in split:
        steps = jnp.exp(jax.random.uniform(jax.random.fold_in(own, position), (shards_of,), jnp.float32, smallest / len(split), largest / len(split)))
        factor_of = factor_of * jnp.repeat(steps, dims[position] // shards_of).reshape([-1 if axis == position else 1 for axis in range(len(dims))])
    return factor_of


def setup_inputs(seed: int = 0) -> dict:
    splits = jax.random.split(jax.random.key(seed), 6)
    start_conc = jnp.clip(jnp.exp(math.log(4.0) - 3.6888794 * jax.random.uniform(splits[0], (ENS, NX, NY, NZ), jnp.float32) ** level_of(splits[0], (ENS, NX, NY, NZ), ((0, 4), (1, 4), (2, 2)), -0.2, 0.2)), 0.1, 4.0)
    target = draw_target(jax.random.fold_in(splits[5], 71), 0)
    log_coef = draw_log_coef(jax.random.fold_in(splits[5], 71), 0)
    inv_temp = jnp.clip(jax.random.uniform(splits[3], (SCHED,), jnp.float32, 1.0, 1.06), 1.0, 1.06)
    sched_start = with_ends(jax.random.randint(splits[4], (ENS,), 0, SCHED - STEPS + 1), jax.random.fold_in(splits[4], 1), 0, SCHED - STEPS).astype(jnp.int32)
    return dict(start_conc=start_conc, target=target, log_coef=log_coef, inv_temp=inv_temp, sched_start=sched_start)


def neighbours(padded):
    padded = jnp.pad(padded, ((0, 0), (0, 0), (1, 1)))
    middle = padded[1:-1, 1:-1, 1:-1]
    near = [padded[2:, 1:-1, 1:-1], padded[:-2, 1:-1, 1:-1],
            padded[1:-1, 2:, 1:-1], padded[1:-1, :-2, 1:-1],
            padded[1:-1, 1:-1, 2:], padded[1:-1, 1:-1, :-2]]
    return middle, near


def diffuse(field_ext, coef_ext):
    field_mid, field_near = neighbours(field_ext)
    coef_mid, coef_near = neighbours(coef_ext)
    result = jnp.zeros_like(field_mid)
    for field_nb, coef_nb in zip(field_near, coef_near):
        result = result + 0.5 * (coef_mid + coef_nb) * (field_nb - field_mid)
    return result


def sensitivity(adjoint_ext, conc_ext):
    adjoint_mid, adjoint_near = neighbours(adjoint_ext)
    conc_mid, conc_near = neighbours(conc_ext)
    result = jnp.zeros_like(conc_mid)
    for adjoint_nb, conc_nb in zip(adjoint_near, conc_near):
        result = result + (adjoint_mid - adjoint_nb) * (conc_mid - conc_nb)
    return -0.5 * result


def pad_sides(field):
    return jnp.pad(field, ((1, 1), (1, 1), (0, 0)))


def reference(start_conc, target, log_coef, inv_temp, sched_start):
    coef = jnp.exp(log_coef)
    coef_ext = pad_sides(coef)
    gradient = jnp.zeros(log_coef.shape, jnp.float32)
    adjoints = []
    finals = []
    for member in range(ENS):
        inverse_temps = lax.dynamic_slice_in_dim(inv_temp, sched_start[member], STEPS)
        rate_list = 0.16 * jnp.exp(4.0 * (1.0 - inverse_temps))
        current = start_conc[member]
        states = []
        for step in range(STEPS):
            padded = pad_sides(current)
            states.append(padded)
            current = current + rate_list[step] * diffuse(padded, coef_ext)
        finals.append(current)
        adjoint = target[member]
        member_grad = jnp.zeros(log_coef.shape, jnp.float32)
        for step in reversed(range(STEPS)):
            padded = pad_sides(adjoint)
            member_grad = member_grad + rate_list[step] * sensitivity(padded, states[step])
            adjoint = adjoint + rate_list[step] * diffuse(padded, coef_ext)
        adjoints.append(adjoint)
        gradient = gradient + member_grad
    return coef * gradient, jnp.stack(adjoints), jnp.stack(finals)
```

```python
import functools
import jax
import jax.numpy as jnp
from jax import lax
from jax.experimental import pallas as pl
from jax.experimental.pallas import tpu as pltpu
from jax.sharding import PartitionSpec as P

STEPS = 4
COEF = 2 * STEPS
ROWS = 32
FAR = -1e30


def body(
    sizes, rates, start, target, logc, grad_out, adj_out, conc_out,
    F, wx, wyp, wym, wz, D, G, E, M,
    load_sem, xs, xr, rs, rr, sa, sb, re, rm,
):
    ngx, nrole = sizes
    nx, ny, nz = logc.shape
    gx, role, ens = lax.axis_index("gx"), lax.axis_index("role"), lax.axis_index("ens")
    main = pl.ds(8, ny)
    lane = lax.broadcasted_iota(jnp.int32, (ROWS, nz), 1)
    first, last = lane == 0, lane == nz - 1
    chunks = range(8, 8 + ny, ROWS)
    is_end = jnp.logical_or(ens == 0, ens == 3)
    is_mid = jnp.logical_and(ens > 0, ens < 3)
    inputs = {0: start.at[0], STEPS: target.at[0], COEF: logc}
    axes = (("gx", gx, ngx), ("role", role, nrole))
    lower = [index > 0 for _, index, _ in axes]
    upper = [index < count - 1 for _, index, count in axes]

    def has_to(axis, d):
        return upper[axis] if d else lower[axis]

    def has_from(axis, d):
        return lower[axis] if d else upper[axis]

    def xcopy(f, d):
        own = nx if d else 1
        src = inputs[f].at[own - 1] if f in inputs else F.at[f, own, main]
        return pltpu.make_async_remote_copy(
            src, F.at[f, 0 if d else nx + 1, main], xs.at[2 * f + d], xr.at[2 * f + d],
            device_id={"gx": gx + (1 if d else -1)}, device_id_type=pl.DeviceIdType.MESH)

    def rcopy(f, d, part, lo, hi):
        planes = pl.ds(lo, hi - lo)
        row = ny - 8 if d else 0
        if f in inputs:
            src = inputs[f].at[:, pl.ds(row, 8)]
        else:
            src = F.at[f, planes, pl.ds(row + 8, 8)]
        sem = (2 * f + d) * 3 + part
        return pltpu.make_async_remote_copy(
            src, F.at[f, planes, pl.ds(0 if d else ny + 8, 8)], rs.at[sem], rr.at[sem],
            device_id={"role": role + (1 if d else -1)}, device_id_type=pl.DeviceIdType.MESH)

    def each(axis, make, do):
        for d in (0, 1):
            cond = has_from(axis, d) if do == "wait_recv" else has_to(axis, d)

            @pl.when(cond)
            def _():
                getattr(make(d), do)()

    def xdo(f, do):
        each(0, lambda d: xcopy(f, d), do)

    def rdo(f, part, lo, hi, do):
        each(1, lambda d: rcopy(f, d, part, lo, hi), do)

    barrier = pltpu.get_barrier_semaphore()
    total = jnp.int32(0)
    for name, index, count in axes + (("ens", ens, 4),):
        for cond, to in ((index > 0, -1), (index < count - 1, 1)):
            total = total + cond.astype(jnp.int32)

            @pl.when(cond)
            def _():
                pl.semaphore_signal(barrier, 1, device_id={name: index + to},
                                    device_id_type=pl.DeviceIdType.MESH)
    loads = [
        pltpu.make_async_copy(inputs[f], F.at[f, pl.ds(1, nx), main], load_sem.at[i])
        for i, f in enumerate((COEF, 0, STEPS))
    ]
    for load in loads:
        load.start()
    pl.semaphore_wait(barrier, total)

    for f in (COEF, 0, STEPS):
        rdo(f, 0, 1, nx + 1, "start")
    for f in (COEF, 0, STEPS):
        xdo(f, "start")

    for side in (0, 1):
        @pl.when(jnp.logical_not(upper[0] if side else lower[0]))
        def _():
            @pl.loop(0, COEF)
            def _(f):
                F[f, (nx + 1) * side, main, :] = jnp.zeros((ny, nz), jnp.float32)
            F[COEF, (nx + 1) * side, main, :] = jnp.full((ny, nz), FAR, jnp.float32)

        @pl.when(jnp.logical_not(upper[1] if side else lower[1]))
        def _():
            edge = pl.ds((ny + 8) * side, 8)

            @pl.loop(0, COEF)
            def _(f):
                F[f, pl.ds(1, nx), edge, :] = jnp.zeros((nx, 8, nz), jnp.float32)
            F[COEF, pl.ds(1, nx), edge, :] = jnp.full((nx, 8, nz), FAR, jnp.float32)

    loads[0].wait()
    rdo(COEF, 0, 1, nx + 1, "wait_recv")

    @pl.loop(1, nx + 1)
    def _(p):
        F[COEF, p] = 0.5 * jnp.exp(F[COEF, p])

    def wx_plane(p):
        wx[p] = F[COEF, p, main, :] + F[COEF, p + 1, main, :]

    def diag_plane(p):
        D[p - 1] = D[p - 1] + (wx[p - 1] + wx[p])

    @pl.loop(1, nx + 1)
    def _(p):
        for y in chunks:
            rows = pl.ds(y - 8, ROWS)
            k = F[COEF, p, pl.ds(y, ROWS), :]
            up = k + F[COEF, p, pl.ds(y + 1, ROWS), :]
            down = k + F[COEF, p, pl.ds(y - 1, ROWS), :]
            right = jnp.where(last, 0.0, k + pltpu.roll(k, nz - 1, 1))
            wyp[p - 1, rows, :] = up
            wym[p - 1, rows, :] = down
            wz[p - 1, rows, :] = right
            D[p - 1, rows, :] = (
                up + down + right + pltpu.roll(right, 1, 1)
                + jnp.where(jnp.logical_or(first, last), k, 0.0))

    pl.loop(1, nx)(wx_plane)
    pl.loop(2, nx)(diag_plane)

    def diffuse(k, lo, hi):
        pairs = ((k, rates[k]), (STEPS + k, rates[STEPS - 1 - k]))

        @pl.loop(lo, hi)
        def _(p):
            for y in chunks:
                rows, here = pl.ds(y - 8, ROWS), pl.ds(y, ROWS)
                w0, w1 = wx[p - 1, rows, :], wx[p, rows, :]
                wp, wm = wyp[p - 1, rows, :], wym[p - 1, rows, :]
                wr, diag = wz[p - 1, rows, :], D[p - 1, rows, :]
                for n, (f, rate) in enumerate(pairs):
                    v = F[f, p, here, :]
                    acc = w0 * F[f, p - 1, here, :] + w1 * F[f, p + 1, here, :]
                    acc = acc + wp * F[f, p, pl.ds(y + 1, ROWS), :]
                    acc = acc + wm * F[f, p, pl.ds(y - 1, ROWS), :]
                    acc = acc + wr * pltpu.roll(v, nz - 1, 1) + pltpu.roll(wr * v, 1, 1)
                    new = v + rate * (acc - diag * v)
                    if k < STEPS - 1:
                        F[f + 1, p, here, :] = new
                    elif n == 0:
                        conc_out[0, p - 1, rows, :] = new
                    else:
                        adj_out[0, p - 1, rows, :] = new

    def sens(p):
        for y in chunks:
            here = pl.ds(y, ROWS)
            up, down = pl.ds(y + 1, ROWS), pl.ds(y - 1, ROWS)
            result = None
            for s in range(STEPS):
                cf, af = s, STEPS + (STEPS - 1 - s)
                c, a = F[cf, p, here, :], F[af, p, here, :]
                acc = (a - F[af, p - 1, here, :]) * (c - F[cf, p - 1, here, :])
                acc = acc + (a - F[af, p + 1, here, :]) * (c - F[cf, p + 1, here, :])
                acc = acc + (a - F[af, p, up, :]) * (c - F[cf, p, up, :])
                acc = acc + (a - F[af, p, down, :]) * (c - F[cf, p, down, :])
                face = (a - jnp.where(last, 0.0, pltpu.roll(a, nz - 1, 1))) * (
                    c - jnp.where(last, 0.0, pltpu.roll(c, nz - 1, 1)))
                acc = acc + face + jnp.where(first, a * c, pltpu.roll(face, 1, 1))
                term = (-0.5 * rates[s]) * acc
                result = term if result is None else result + term
            G[p - 1, pl.ds(y - 8, ROWS), :] = result

    def ens_copy(src, dst, send, recv, to):
        return pltpu.make_async_remote_copy(
            src, dst, send, recv, device_id={"ens": to}, device_id_type=pl.DeviceIdType.MESH)

    quarter = nx // 4

    def plane(i):
        return lax.rem(i + quarter, nx)

    def end_send(i):
        q = plane(i)
        return ens_copy(G.at[q], E.at[q], sa.at[i], re.at[i], 1 + ens // 3)

    def peer_send(i):
        q = plane(i)
        return ens_copy(E.at[q], M.at[q], sa.at[i], rm.at[i], 3 - ens)

    def back_send(i):
        q = plane(i)
        return ens_copy(G.at[q], M.at[q], sb.at[i], rm.at[i], (ens - 1) * 3)

    def gradient(lo, hi):
        @pl.loop(lo, hi)
        def _(i):
            sens(plane(i) + 1)

            @pl.when(is_end)
            def _():
                end_send(i).start()

    def merge(lo, hi):
        @pl.when(is_mid)
        def _():
            @pl.loop(lo, hi)
            def _(i):
                q = plane(i)
                end_send(i).wait_recv()
                E[q] = E[q] + G[q]
                peer_send(i).start()

    def close(lo, hi):
        @pl.when(is_mid)
        def _():
            @pl.loop(lo, hi)
            def _(i):
                q = plane(i)
                peer_send(i).wait_recv()
                G[q] = E[q] + M[q]
                back_send(i).start()
                grad_out[q] = 2.0 * F[COEF, q + 1, main, :] * G[q]

    def finish(lo, hi):
        @pl.when(is_end)
        def _():
            @pl.loop(lo, hi)
            def _(i):
                q = plane(i)
                back_send(i).wait_recv()
                grad_out[q] = 2.0 * F[COEF, q + 1, main, :] * M[q]

    loads[1].wait()
    loads[2].wait()
    for f in (0, STEPS):
        rdo(f, 0, 1, nx + 1, "wait_recv")
    for k in range(STEPS - 1):
        lo, hi = k + 2, nx - k
        diffuse(k, lo, hi)
        for f in (k + 1, STEPS + k + 1):
            rdo(f, 0, lo, hi, "start")
        if k == 0:
            xdo(COEF, "wait_recv")
            for p in (0, nx + 1):
                F[COEF, p, main, :] = 0.5 * jnp.exp(F[COEF, p, main, :])
            wx_plane(0)
            wx_plane(nx)
            diag_plane(1)
            diag_plane(nx)
        for f in (k + 1, STEPS + k + 1):
            rdo(f, 0, lo, hi, "wait_recv")
    gradient(0, nx // 2)

    half = nx // 2
    third = half // 3
    for k in range(STEPS):
        for f in (k, STEPS + k):
            xdo(f, "wait_recv")
            if k > 0:
                rdo(f, 1, 1, k + 1, "wait_recv")
                rdo(f, 2, nx + 1 - k, nx + 1, "wait_recv")
        if k < STEPS - 1:
            diffuse(k, 1, k + 2)
            diffuse(k, nx - k, nx + 1)
            for f in (k + 1, STEPS + k + 1):
                xdo(f, "start")
                rdo(f, 1, 1, k + 2, "start")
                rdo(f, 2, nx - k, nx + 1, "start")
            if k == 0:
                merge(0, half // 2)
                diffuse(STEPS - 1, quarter + 1, nx - quarter + 1)
            elif k == 1:
                merge(half // 2, half)
                close(0, half // 2)
            else:
                close(half // 2, half)
    gradient(half, nx)
    merge(half, half + 2)
    diffuse(STEPS - 1, 1, quarter + 1)
    merge(half + 2, nx)
    diffuse(STEPS - 1, nx - quarter + 1, nx + 1)
    close(half, nx)
    finish(0, nx)

    for f in range(COEF + 1):
        xdo(f, "wait_send")
        k = f % STEPS
        if f in inputs:
            rdo(f, 0, 1, nx + 1, "wait_send")
        else:
            rdo(f, 0, k + 1, nx + 1 - k, "wait_send")
            rdo(f, 1, 1, k + 1, "wait_send")
            rdo(f, 2, nx + 1 - k, nx + 1, "wait_send")

    @pl.loop(0, nx)
    def _(i):
        @pl.when(is_end)
        def _():
            end_send(i).wait_send()

        @pl.when(is_mid)
        def _():
            peer_send(i).wait_send()
            back_send(i).wait_send()


def shards(sizes, start_conc, target, log_coef, inv_temp, sched_start):
    inverse_temps = lax.dynamic_slice_in_dim(inv_temp, sched_start[0], STEPS)
    rates = 0.16 * jnp.exp(4.0 * (1.0 - inverse_temps))
    nx, ny, nz = log_coef.shape
    f32 = jnp.float32
    field = pltpu.VMEM((nx, ny, nz), f32)
    dma = pltpu.SemaphoreType.DMA
    fields = COEF + 1
    vmem = pl.BlockSpec(memory_space=pltpu.VMEM)
    hbm = pl.BlockSpec(memory_space=pl.ANY)
    return pl.pallas_call(
        functools.partial(body, sizes),
        out_shape=(
            jax.ShapeDtypeStruct(log_coef.shape, f32),
            jax.ShapeDtypeStruct(start_conc.shape, f32),
            jax.ShapeDtypeStruct(start_conc.shape, f32),
        ),
        in_specs=[pl.BlockSpec(memory_space=pltpu.SMEM), hbm, hbm, hbm],
        out_specs=(vmem, vmem, vmem),
        scratch_shapes=[
            pltpu.VMEM((fields, nx + 2, ny + 16, nz), f32),
            pltpu.VMEM((nx + 1, ny, nz), f32),
            field, field, field, field, field, field, field,
            dma((3,)), dma((2 * fields,)), dma((2 * fields,)),
            dma((6 * fields,)), dma((6 * fields,)),
            dma((nx,)), dma((nx,)), dma((nx,)), dma((nx,)),
        ],
        compiler_params=pltpu.CompilerParams(
            collective_id=0, has_side_effects=True, vmem_limit_bytes=60 * 1024 * 1024),
    )(rates, start_conc, target, log_coef)


def solution(mesh):
    placed = (
        P("ens", "gx", "role", None),
        P("ens", "gx", "role", None),
        P("gx", "role", None),
        P(),
        P("ens"),
    )
    return jax.shard_map(
        functools.partial(shards, (mesh.shape["gx"], mesh.shape["role"])),
        mesh=mesh,
        in_specs=placed,
        out_specs=(
            P("gx", "role", None),
            P("ens", "gx", "role", None),
            P("ens", "gx", "role", None),
        ),
        check_vma=False,
    )
```

```python
import functools
import jax
import jax.numpy as jnp
from jax import lax
from jax.experimental import pallas as pl
from jax.experimental.pallas import tpu as pltpu
from jax.sharding import PartitionSpec as P

STEPS = 4
COEF = 2 * STEPS
ROWS = 32
FAR = -1e30


def body(
    sizes, rates, start, target, logc, grad_out, adj_out, conc_out,
    F, wx, wyp, wym, wz, D, G, E, M, FX, FY,
    load_sem, xs, xr, rs, rr, sa, sb, re, rm,
):
    ngx, nrole = sizes
    nx, ny, nz = logc.shape
    gx, role, ens = lax.axis_index("gx"), lax.axis_index("role"), lax.axis_index("ens")
    main = pl.ds(8, ny)
    lane = lax.broadcasted_iota(jnp.int32, (ROWS, nz), 1)
    first, last = lane == 0, lane == nz - 1
    chunks = range(8, 8 + ny, ROWS)
    is_end = jnp.logical_or(ens == 0, ens == 3)
    is_mid = jnp.logical_and(ens > 0, ens < 3)
    inputs = {0: start.at[0], STEPS: target.at[0], COEF: logc}
    axes = (("gx", gx, ngx), ("role", role, nrole))
    lower = [index > 0 for _, index, _ in axes]
    upper = [index < count - 1 for _, index, count in axes]

    def has_to(axis, d):
        return upper[axis] if d else lower[axis]

    def has_from(axis, d):
        return lower[axis] if d else upper[axis]

    def xcopy(f, d):
        own = nx if d else 1
        src = inputs[f].at[own - 1] if f in inputs else F.at[f, own, main]
        return pltpu.make_async_remote_copy(
            src, F.at[f, 0 if d else nx + 1, main], xs.at[2 * f + d], xr.at[2 * f + d],
            device_id={"gx": gx + (1 if d else -1)}, device_id_type=pl.DeviceIdType.MESH)

    def rcopy(f, d, part, lo, hi):
        planes = pl.ds(lo, hi - lo)
        row = ny - 8 if d else 0
        if f in inputs:
            src = inputs[f].at[:, pl.ds(row, 8)]
        else:
            src = F.at[f, planes, pl.ds(row + 8, 8)]
        sem = (2 * f + d) * 3 + part
        return pltpu.make_async_remote_copy(
            src, F.at[f, planes, pl.ds(0 if d else ny + 8, 8)], rs.at[sem], rr.at[sem],
            device_id={"role": role + (1 if d else -1)}, device_id_type=pl.DeviceIdType.MESH)

    def each(axis, make, do):
        for d in (0, 1):
            cond = has_from(axis, d) if do == "wait_recv" else has_to(axis, d)

            @pl.when(cond)
            def _():
                getattr(make(d), do)()

    def xdo(f, do):
        each(0, lambda d: xcopy(f, d), do)

    def rdo(f, part, lo, hi, do):
        each(1, lambda d: rcopy(f, d, part, lo, hi), do)

    barrier = pltpu.get_barrier_semaphore()
    total = jnp.int32(0)
    for name, index, count in axes + (("ens", ens, 4),):
        for cond, to in ((index > 0, -1), (index < count - 1, 1)):
            total = total + cond.astype(jnp.int32)

            @pl.when(cond)
            def _():
                pl.semaphore_signal(barrier, 1, device_id={name: index + to},
                                    device_id_type=pl.DeviceIdType.MESH)
    loads = [
        pltpu.make_async_copy(inputs[f], F.at[f, pl.ds(1, nx), main], load_sem.at[i])
        for i, f in enumerate((COEF, 0, STEPS))
    ]
    for load in loads:
        load.start()
    pl.semaphore_wait(barrier, total)

    for f in (COEF, 0, STEPS):
        rdo(f, 0, 1, nx + 1, "start")
    for f in (COEF, 0, STEPS):
        xdo(f, "start")

    for side in (0, 1):
        @pl.when(jnp.logical_not(upper[0] if side else lower[0]))
        def _():
            @pl.loop(0, COEF)
            def _(f):
                F[f, (nx + 1) * side, main, :] = jnp.zeros((ny, nz), jnp.float32)
            F[COEF, (nx + 1) * side, main, :] = jnp.full((ny, nz), FAR, jnp.float32)

        @pl.when(jnp.logical_not(upper[1] if side else lower[1]))
        def _():
            edge = pl.ds((ny + 8) * side, 8)

            @pl.loop(0, COEF)
            def _(f):
                F[f, pl.ds(1, nx), edge, :] = jnp.zeros((nx, 8, nz), jnp.float32)
            F[COEF, pl.ds(1, nx), edge, :] = jnp.full((nx, 8, nz), FAR, jnp.float32)

    loads[0].wait()
    rdo(COEF, 0, 1, nx + 1, "wait_recv")

    @pl.loop(1, nx + 1)
    def _(p):
        F[COEF, p] = 0.5 * jnp.exp(F[COEF, p])

    def wx_plane(p):
        wx[p] = F[COEF, p, main, :] + F[COEF, p + 1, main, :]

    def diag_plane(p):
        D[p - 1] = D[p - 1] + (wx[p - 1] + wx[p])

    @pl.loop(1, nx + 1)
    def _(p):
        for y in chunks:
            rows = pl.ds(y - 8, ROWS)
            k = F[COEF, p, pl.ds(y, ROWS), :]
            up = k + F[COEF, p, pl.ds(y + 1, ROWS), :]
            down = k + F[COEF, p, pl.ds(y - 1, ROWS), :]
            right = jnp.where(last, 0.0, k + pltpu.roll(k, nz - 1, 1))
            wyp[p - 1, rows, :] = up
            wym[p - 1, rows, :] = down
            wz[p - 1, rows, :] = right
            D[p - 1, rows, :] = (
                up + down + right + pltpu.roll(right, 1, 1)
                + jnp.where(jnp.logical_or(first, last), k, 0.0))

    pl.loop(1, nx)(wx_plane)
    pl.loop(2, nx)(diag_plane)

    def diffuse(k, lo, hi):
        pairs = ((k, rates[k]), (STEPS + k, rates[STEPS - 1 - k]))

        @pl.loop(lo, hi)
        def _(p):
            for y in chunks:
                rows, here = pl.ds(y - 8, ROWS), pl.ds(y, ROWS)
                w0, w1 = wx[p - 1, rows, :], wx[p, rows, :]
                wp, wm = wyp[p - 1, rows, :], wym[p - 1, rows, :]
                wr, diag = wz[p - 1, rows, :], D[p - 1, rows, :]
                for n, (f, rate) in enumerate(pairs):
                    wide = F[f, p, pl.ds(y - 8, ROWS + 16), :]
                    v = wide[8:8 + ROWS]
                    acc = w0 * F[f, p - 1, here, :] + w1 * F[f, p + 1, here, :]
                    acc = acc + wp * wide[9:9 + ROWS]
                    acc = acc + wm * wide[7:7 + ROWS]
                    acc = acc + wr * pltpu.roll(v, nz - 1, 1) + pltpu.roll(wr * v, 1, 1)
                    new = v + rate * (acc - diag * v)
                    if k < STEPS - 1:
                        F[f + 1, p, here, :] = new
                    elif n == 0:
                        conc_out[0, p - 1, rows, :] = new
                    else:
                        adj_out[0, p - 1, rows, :] = new

    def face_x(p):
        for y in chunks:
            here = pl.ds(y, ROWS)
            total_x = 0.0
            for s in range(STEPS):
                cf, af = s, STEPS + (STEPS - 1 - s)
                da = F[af, p, here, :] - F[af, p + 1, here, :]
                dc = F[cf, p, here, :] - F[cf, p + 1, here, :]
                total_x = total_x + rates[s] * (da * dc)
            FX[p, pl.ds(y - 8, ROWS), :] = total_x

    def sens(p):
        edge_y = 0.0
        for s in range(STEPS):
            cf, af = s, STEPS + (STEPS - 1 - s)
            da = F[af, p, pl.ds(0, 8), :] - F[af, p, pl.ds(1, 8), :]
            dc = F[cf, p, pl.ds(0, 8), :] - F[cf, p, pl.ds(1, 8), :]
            edge_y = edge_y + rates[s] * (da * dc)
        FY[pl.ds(0, 8), :] = edge_y
        for y in chunks:
            here, up = pl.ds(y, ROWS), pl.ds(y + 1, ROWS)
            rows = pl.ds(y - 8, ROWS)
            tx, ty, tz, t0 = 0.0, 0.0, 0.0, 0.0
            for s in range(STEPS):
                cf, af = s, STEPS + (STEPS - 1 - s)
                c, a = F[cf, p, here, :], F[af, p, here, :]
                tx = tx + rates[s] * ((a - F[af, p + 1, here, :]) * (c - F[cf, p + 1, here, :]))
                ty = ty + rates[s] * ((a - F[af, p, up, :]) * (c - F[cf, p, up, :]))
                da = a - jnp.where(last, 0.0, pltpu.roll(a, nz - 1, 1))
                dc = c - jnp.where(last, 0.0, pltpu.roll(c, nz - 1, 1))
                tz = tz + rates[s] * (da * dc)
                t0 = t0 + rates[s] * (a[:, :128] * c[:, :128])
            FX[p, rows, :] = tx
            FY[here, :] = ty
            low_z = jnp.where(first, jnp.concatenate([t0] * (nz // 128), axis=1), pltpu.roll(tz, 1, 1))
            low_y = FY[pl.ds(y - 1, ROWS), :]
            G[p - 1, rows, :] = -0.5 * ((tx + FX[p - 1, rows, :]) + (ty + low_y) + (tz + low_z))

    def ens_copy(src, dst, send, recv, to):
        return pltpu.make_async_remote_copy(
            src, dst, send, recv, device_id={"ens": to}, device_id_type=pl.DeviceIdType.MESH)

    quarter = nx // 4

    def plane(i):
        return lax.rem(i + quarter, nx)

    def end_send(i):
        q = plane(i)
        return ens_copy(G.at[q], E.at[q], sa.at[i], re.at[i], 1 + ens // 3)

    def peer_send(i):
        q = plane(i)
        return ens_copy(E.at[q], M.at[q], sa.at[i], rm.at[i], 3 - ens)

    def back_send(i):
        q = plane(i)
        return ens_copy(G.at[q], M.at[q], sb.at[i], rm.at[i], (ens - 1) * 3)

    def gradient(lo, hi):
        @pl.loop(lo, hi)
        def _(i):
            sens(plane(i) + 1)

            @pl.when(is_end)
            def _():
                end_send(i).start()

    def merge_one(i):
        q = plane(i)
        end_send(i).wait_recv()
        E[q] = E[q] + G[q]
        peer_send(i).start()

    def close_one(i):
        q = plane(i)
        peer_send(i).wait_recv()
        G[q] = E[q] + M[q]
        back_send(i).start()
        grad_out[q] = 2.0 * F[COEF, q + 1, main, :] * G[q]

    def merge(lo, hi):
        @pl.when(is_mid)
        def _():
            pl.loop(lo, hi)(merge_one)

    def close(lo, hi):
        @pl.when(is_mid)
        def _():
            pl.loop(lo, hi)(close_one)

    def finish(lo, hi):
        @pl.when(is_end)
        def _():
            @pl.loop(lo, hi)
            def _(i):
                q = plane(i)
                back_send(i).wait_recv()
                grad_out[q] = 2.0 * F[COEF, q + 1, main, :] * M[q]

    loads[1].wait()
    loads[2].wait()
    for f in (0, STEPS):
        rdo(f, 0, 1, nx + 1, "wait_recv")
    half = nx // 2

    def inner(k):
        lo, hi = k + 2, nx - k
        if k > 0:
            for f in (k, STEPS + k):
                rdo(f, 0, lo - 1, hi + 1, "wait_recv")
        diffuse(k, lo, hi)
        for f in (k + 1, STEPS + k + 1):
            rdo(f, 0, lo, hi, "start")

    def arrive(k):
        for f in (k, STEPS + k):
            xdo(f, "wait_recv")
            if k > 0:
                rdo(f, 1, 1, k + 1, "wait_recv")
                rdo(f, 2, nx + 1 - k, nx + 1, "wait_recv")

    def outer(k):
        arrive(k)
        for lo, hi in ((1, 2), (nx, nx + 1)):
            diffuse(k, lo, hi)
        for f in (k + 1, STEPS + k + 1):
            xdo(f, "start")
        if k > 0:
            diffuse(k, 2, k + 2)
            diffuse(k, nx - k, nx)
        for f in (k + 1, STEPS + k + 1):
            rdo(f, 1, 1, k + 2, "start")
            rdo(f, 2, nx - k, nx + 1, "start")

    inner(0)
    xdo(COEF, "wait_recv")
    for p in (0, nx + 1):
        F[COEF, p, main, :] = 0.5 * jnp.exp(F[COEF, p, main, :])
    wx_plane(0)
    wx_plane(nx)
    diag_plane(1)
    diag_plane(nx)
    inner(1)
    outer(0)
    inner(2)
    for f in (STEPS - 1, COEF - 1):
        rdo(f, 0, STEPS, nx - STEPS + 2, "wait_recv")
    face_x(quarter)
    gradient(0, half)
    outer(1)
    merge(0, 2)
    diffuse(STEPS - 1, quarter + 1, nx - quarter + 1)
    merge(2, 4)
    close(0, 2)
    outer(2)
    merge(4, half)
    close(2, 5)
    arrive(STEPS - 1)
    face_x(0)
    gradient(half, nx)
    close(5, half)
    diffuse(STEPS - 1, 1, quarter + 1)
    merge(half, half + 1)
    diffuse(STEPS - 1, nx - quarter + 1, nx + 1)
    merge(half + 1, half + 2)

    @pl.when(is_mid)
    def _():
        @pl.loop(half + 2, nx)
        def _(i):
            merge_one(i)
            close_one(i - 2)
    close(nx - 2, nx)
    finish(0, nx)

    for f in range(COEF + 1):
        xdo(f, "wait_send")
        k = f % STEPS
        if f in inputs:
            rdo(f, 0, 1, nx + 1, "wait_send")
        else:
            rdo(f, 0, k + 1, nx + 1 - k, "wait_send")
            rdo(f, 1, 1, k + 1, "wait_send")
            rdo(f, 2, nx + 1 - k, nx + 1, "wait_send")

    @pl.loop(0, nx)
    def _(i):
        @pl.when(is_end)
        def _():
            end_send(i).wait_send()

        @pl.when(is_mid)
        def _():
            peer_send(i).wait_send()
            back_send(i).wait_send()


def shards(sizes, start_conc, target, log_coef, inv_temp, sched_start):
    inverse_temps = lax.dynamic_slice_in_dim(inv_temp, sched_start[0], STEPS)
    rates = 0.16 * jnp.exp(4.0 * (1.0 - inverse_temps))
    nx, ny, nz = log_coef.shape
    f32 = jnp.float32
    field = pltpu.VMEM((nx, ny, nz), f32)
    dma = pltpu.SemaphoreType.DMA
    fields = COEF + 1
    vmem = pl.BlockSpec(memory_space=pltpu.VMEM)
    hbm = pl.BlockSpec(memory_space=pl.ANY)
    return pl.pallas_call(
        functools.partial(body, sizes),
        out_shape=(
            jax.ShapeDtypeStruct(log_coef.shape, f32),
            jax.ShapeDtypeStruct(start_conc.shape, f32),
            jax.ShapeDtypeStruct(start_conc.shape, f32),
        ),
        in_specs=[pl.BlockSpec(memory_space=pltpu.SMEM), hbm, hbm, hbm],
        out_specs=(vmem, vmem, vmem),
        scratch_shapes=[
            pltpu.VMEM((fields, nx + 2, ny + 16, nz), f32),
            pltpu.VMEM((nx + 1, ny, nz), f32),
            field, field, field, field, field, field, field,
            pltpu.VMEM((nx + 1, ny, nz), f32), pltpu.VMEM((ny + 16, nz), f32),
            dma((3,)), dma((2 * fields,)), dma((2 * fields,)),
            dma((6 * fields,)), dma((6 * fields,)),
            dma((nx,)), dma((nx,)), dma((nx,)), dma((nx,)),
        ],
        compiler_params=pltpu.CompilerParams(
            collective_id=0, has_side_effects=True, vmem_limit_bytes=60 * 1024 * 1024),
    )(rates, start_conc, target, log_coef)


def solution(mesh):
    placed = (
        P("ens", "gx", "role", None),
        P("ens", "gx", "role", None),
        P("gx", "role", None),
        P(),
        P("ens"),
    )
    return jax.shard_map(
        functools.partial(shards, (mesh.shape["gx"], mesh.shape["role"])),
        mesh=mesh,
        in_specs=placed,
        out_specs=(
            P("gx", "role", None),
            P("ens", "gx", "role", None),
            P("ens", "gx", "role", None),
        ),
        check_vma=False,
    )
```

```python
import functools
import jax
import jax.numpy as jnp
from jax import lax
from jax.experimental import pallas as pl
from jax.experimental.pallas import tpu as pltpu
from jax.sharding import PartitionSpec as P

STEPS = 4
COEF = 2 * STEPS
PARTS = 2 * STEPS - 1
ROWS = 32
FAR = -1e30


def body(
    sizes, rates, start, target, logc, grad_out, adj_out, conc_out,
    F, wx, wyp, wym, wz, D, G, E, M, FX, FY,
    load_sem, xs, xr, rs, rr, sa, sb, re, rm,
):
    ngx, nrole = sizes
    nx, ny, nz = logc.shape
    gx, role, ens = lax.axis_index("gx"), lax.axis_index("role"), lax.axis_index("ens")
    main = pl.ds(8, ny)
    lane = lax.broadcasted_iota(jnp.int32, (ROWS, nz), 1)
    first, last = lane == 0, lane == nz - 1
    chunks = range(8, 8 + ny, ROWS)
    is_end = jnp.logical_or(ens == 0, ens == 3)
    is_mid = jnp.logical_and(ens > 0, ens < 3)
    inputs = {0: start.at[0], STEPS: target.at[0], COEF: logc}
    axes = (("gx", gx, ngx), ("role", role, nrole))
    lower = [index > 0 for _, index, _ in axes]
    upper = [index < count - 1 for _, index, count in axes]

    def has_to(axis, d):
        return upper[axis] if d else lower[axis]

    def has_from(axis, d):
        return lower[axis] if d else upper[axis]

    def xcopy(f, d):
        own = nx if d else 1
        src = inputs[f].at[own - 1] if f in inputs else F.at[f, own, main]
        return pltpu.make_async_remote_copy(
            src, F.at[f, 0 if d else nx + 1, main], xs.at[2 * f + d], xr.at[2 * f + d],
            device_id={"gx": gx + (1 if d else -1)}, device_id_type=pl.DeviceIdType.MESH)

    def rcopy(f, d, part, lo, hi):
        planes = pl.ds(lo, hi - lo)
        row = ny - 8 if d else 0
        if f in inputs:
            src = inputs[f].at[:, pl.ds(row, 8)]
        else:
            src = F.at[f, planes, pl.ds(row + 8, 8)]
        sem = (2 * f + d) * PARTS + part
        return pltpu.make_async_remote_copy(
            src, F.at[f, planes, pl.ds(0 if d else ny + 8, 8)], rs.at[sem], rr.at[sem],
            device_id={"role": role + (1 if d else -1)}, device_id_type=pl.DeviceIdType.MESH)

    def each(axis, make, do):
        for d in (0, 1):
            cond = has_from(axis, d) if do == "wait_recv" else has_to(axis, d)

            @pl.when(cond)
            def _():
                getattr(make(d), do)()

    def xdo(f, do):
        each(0, lambda d: xcopy(f, d), do)

    def rdo(f, part, lo, hi, do):
        each(1, lambda d: rcopy(f, d, part, lo, hi), do)

    barrier = pltpu.get_barrier_semaphore()
    total = jnp.int32(0)
    for name, index, count in axes + (("ens", ens, 4),):
        for cond, to in ((index > 0, -1), (index < count - 1, 1)):
            total = total + cond.astype(jnp.int32)

            @pl.when(cond)
            def _():
                pl.semaphore_signal(barrier, 1, device_id={name: index + to},
                                    device_id_type=pl.DeviceIdType.MESH)
    loads = [
        pltpu.make_async_copy(inputs[f], F.at[f, pl.ds(1, nx), main], load_sem.at[i])
        for i, f in enumerate((COEF, 0, STEPS))
    ]
    for load in loads:
        load.start()
    pl.semaphore_wait(barrier, total)

    for f in (COEF, 0, STEPS):
        rdo(f, 0, 1, nx + 1, "start")
    for f in (COEF, 0, STEPS):
        xdo(f, "start")

    for side in (0, 1):
        @pl.when(jnp.logical_not(upper[0] if side else lower[0]))
        def _():
            @pl.loop(0, COEF)
            def _(f):
                F[f, (nx + 1) * side, main, :] = jnp.zeros((ny, nz), jnp.float32)
            F[COEF, (nx + 1) * side, main, :] = jnp.full((ny, nz), FAR, jnp.float32)

        @pl.when(jnp.logical_not(upper[1] if side else lower[1]))
        def _():
            edge = pl.ds((ny + 8) * side, 8)

            @pl.loop(0, COEF)
            def _(f):
                F[f, pl.ds(1, nx), edge, :] = jnp.zeros((nx, 8, nz), jnp.float32)
            F[COEF, pl.ds(1, nx), edge, :] = jnp.full((nx, 8, nz), FAR, jnp.float32)

    loads[0].wait()
    rdo(COEF, 0, 1, nx + 1, "wait_recv")

    @pl.loop(1, nx + 1)
    def _(p):
        F[COEF, p] = 0.5 * jnp.exp(F[COEF, p])

    def wx_plane(p):
        wx[p] = F[COEF, p, main, :] + F[COEF, p + 1, main, :]

    def diag_plane(p):
        D[p - 1] = D[p - 1] + (wx[p - 1] + wx[p])

    @pl.loop(1, nx + 1)
    def _(p):
        for y in chunks:
            rows = pl.ds(y - 8, ROWS)
            k = F[COEF, p, pl.ds(y, ROWS), :]
            up = k + F[COEF, p, pl.ds(y + 1, ROWS), :]
            down = k + F[COEF, p, pl.ds(y - 1, ROWS), :]
            right = jnp.where(last, 0.0, k + pltpu.roll(k, nz - 1, 1))
            wyp[p - 1, rows, :] = up
            wym[p - 1, rows, :] = down
            wz[p - 1, rows, :] = right
            D[p - 1, rows, :] = (
                up + down + right + pltpu.roll(right, 1, 1)
                + jnp.where(jnp.logical_or(first, last), k, 0.0))

    pl.loop(1, nx)(wx_plane)
    pl.loop(2, nx)(diag_plane)

    def diffuse(k, lo, hi):
        pairs = ((k, rates[k]), (STEPS + k, rates[STEPS - 1 - k]))

        @pl.loop(lo, hi)
        def _(p):
            for y in chunks:
                rows, here = pl.ds(y - 8, ROWS), pl.ds(y, ROWS)
                w0, w1 = wx[p - 1, rows, :], wx[p, rows, :]
                wp, wm = wyp[p - 1, rows, :], wym[p - 1, rows, :]
                wr, diag = wz[p - 1, rows, :], D[p - 1, rows, :]
                for n, (f, rate) in enumerate(pairs):
                    wide = F[f, p, pl.ds(y - 8, ROWS + 16), :]
                    v = wide[8:8 + ROWS]
                    acc = w0 * F[f, p - 1, here, :] + w1 * F[f, p + 1, here, :]
                    acc = acc + wp * wide[9:9 + ROWS]
                    acc = acc + wm * wide[7:7 + ROWS]
                    acc = acc + wr * pltpu.roll(v, nz - 1, 1) + pltpu.roll(wr * v, 1, 1)
                    new = v + rate * (acc - diag * v)
                    if k < STEPS - 1:
                        F[f + 1, p, here, :] = new
                    elif n == 0:
                        conc_out[0, p - 1, rows, :] = new
                    else:
                        adj_out[0, p - 1, rows, :] = new

    def face_x(p):
        for y in chunks:
            here = pl.ds(y, ROWS)
            total_x = 0.0
            for s in range(STEPS):
                cf, af = s, STEPS + (STEPS - 1 - s)
                da = F[af, p, here, :] - F[af, p + 1, here, :]
                dc = F[cf, p, here, :] - F[cf, p + 1, here, :]
                total_x = total_x + rates[s] * (da * dc)
            FX[p, pl.ds(y - 8, ROWS), :] = total_x

    def sens(p):
        edge_y = 0.0
        for s in range(STEPS):
            cf, af = s, STEPS + (STEPS - 1 - s)
            da = F[af, p, pl.ds(0, 8), :] - F[af, p, pl.ds(1, 8), :]
            dc = F[cf, p, pl.ds(0, 8), :] - F[cf, p, pl.ds(1, 8), :]
            edge_y = edge_y + rates[s] * (da * dc)
        FY[pl.ds(0, 8), :] = edge_y
        for y in chunks:
            here, up = pl.ds(y, ROWS), pl.ds(y + 1, ROWS)
            rows = pl.ds(y - 8, ROWS)
            tx, ty, tz, t0 = 0.0, 0.0, 0.0, 0.0
            for s in range(STEPS):
                cf, af = s, STEPS + (STEPS - 1 - s)
                c, a = F[cf, p, here, :], F[af, p, here, :]
                tx = tx + rates[s] * ((a - F[af, p + 1, here, :]) * (c - F[cf, p + 1, here, :]))
                ty = ty + rates[s] * ((a - F[af, p, up, :]) * (c - F[cf, p, up, :]))
                da = a - jnp.where(last, 0.0, pltpu.roll(a, nz - 1, 1))
                dc = c - jnp.where(last, 0.0, pltpu.roll(c, nz - 1, 1))
                tz = tz + rates[s] * (da * dc)
                t0 = t0 + rates[s] * (a[:, :128] * c[:, :128])
            FX[p, rows, :] = tx
            FY[here, :] = ty
            low_z = jnp.where(first, jnp.concatenate([t0] * (nz // 128), axis=1), pltpu.roll(tz, 1, 1))
            low_y = FY[pl.ds(y - 1, ROWS), :]
            G[p - 1, rows, :] = -0.5 * ((tx + FX[p - 1, rows, :]) + (ty + low_y) + (tz + low_z))

    def ens_copy(src, dst, send, recv, to):
        return pltpu.make_async_remote_copy(
            src, dst, send, recv, device_id={"ens": to}, device_id_type=pl.DeviceIdType.MESH)

    quarter, half = STEPS, nx - 2 * STEPS

    def plane(i):
        outside, side, ring = lax.div(i, half), lax.rem(i, 2), lax.div(i, 2) - half // 2
        pair = quarter - 1 - ring + side * (half + 1 + 2 * ring)
        return (1 - outside) * (i + quarter) + outside * pair

    def end_send(i):
        q = plane(i)
        return ens_copy(G.at[q], E.at[q], sa.at[i], re.at[i], 1 + ens // 3)

    def peer_send(i):
        q = plane(i)
        return ens_copy(E.at[q], M.at[q], sa.at[i], rm.at[i], 3 - ens)

    def back_send(i):
        q = plane(i)
        return ens_copy(G.at[q], M.at[q], sb.at[i], rm.at[i], (ens - 1) * 3)

    def gradient(lo, hi):
        @pl.loop(lo, hi)
        def _(i):
            sens(plane(i) + 1)

            @pl.when(is_end)
            def _():
                end_send(i).start()

    def merge_one(i):
        q = plane(i)
        end_send(i).wait_recv()
        E[q] = E[q] + G[q]
        peer_send(i).start()

    def close_one(i):
        q = plane(i)
        peer_send(i).wait_recv()
        G[q] = E[q] + M[q]
        back_send(i).start()
        grad_out[q] = 2.0 * F[COEF, q + 1, main, :] * G[q]

    def merge(lo, hi):
        @pl.when(is_mid)
        def _():
            pl.loop(lo, hi)(merge_one)

    def close(lo, hi):
        @pl.when(is_mid)
        def _():
            pl.loop(lo, hi)(close_one)

    def finish(lo, hi):
        @pl.when(is_end)
        def _():
            @pl.loop(lo, hi)
            def _(i):
                q = plane(i)
                back_send(i).wait_recv()
                grad_out[q] = 2.0 * F[COEF, q + 1, main, :] * M[q]

    loads[1].wait()
    loads[2].wait()
    for f in (0, STEPS):
        rdo(f, 0, 1, nx + 1, "wait_recv")
    def inner(k):
        lo, hi = k + 2, nx - k
        if k > 0:
            for f in (k, STEPS + k):
                rdo(f, 0, lo - 1, hi + 1, "wait_recv")
        diffuse(k, lo, hi)
        for f in (k + 1, STEPS + k + 1):
            rdo(f, 0, lo, hi, "start")

    def single(level, q, do):
        for f in (level, STEPS + level):
            rdo(f, 2 * q - 1, q, q + 1, do)
            rdo(f, 2 * q, nx + 1 - q, nx + 2 - q, do)

    def arrive(k):
        for f in (k, STEPS + k):
            xdo(f, "wait_recv")
        for level in range(max(k, 1), STEPS):
            if k > 0:
                single(level, level - k + 1, "wait_recv")

    def wave(k, j):
        q = j - k + 1
        diffuse(j, q, q + 1)
        diffuse(j, nx + 1 - q, nx + 2 - q)
        if j == k:
            for f in (k + 1, STEPS + k + 1):
                xdo(f, "start")
        single(j + 1, q, "start")

    def ring(k):
        face_x(quarter - k - 1)
        gradient(half + 2 * k, half + 2 * k + 2)

    inner(0)
    xdo(COEF, "wait_recv")
    for p in (0, nx + 1):
        F[COEF, p, main, :] = 0.5 * jnp.exp(F[COEF, p, main, :])
    wx_plane(0)
    wx_plane(nx)
    diag_plane(1)
    diag_plane(nx)
    inner(1)
    arrive(0)
    wave(0, 0)
    inner(2)
    for f in (STEPS - 1, COEF - 1):
        rdo(f, 0, STEPS, nx - STEPS + 2, "wait_recv")
    face_x(quarter)
    gradient(0, half)
    wave(0, 1)
    wave(0, 2)
    ring(0)
    arrive(1)
    wave(1, 1)
    wave(1, 2)
    ring(1)
    merge(0, 3)
    diffuse(STEPS - 1, quarter + 1, nx - quarter + 1)
    merge(3, 5)
    close(0, 2)
    arrive(2)
    wave(2, 2)
    ring(2)
    merge(5, half)
    close(2, 5)
    arrive(3)
    ring(3)
    merge(half, half + 1)
    close(5, 7)
    diffuse(STEPS - 1, 1, quarter + 1)
    merge(half + 1, half + 2)
    close(7, half)
    diffuse(STEPS - 1, nx - quarter + 1, nx + 1)

    @pl.when(is_mid)
    def _():
        @pl.loop(half + 2, nx)
        def _(i):
            merge_one(i)
            close_one(i - 2)
    close(nx - 2, nx)
    finish(0, nx)

    for f in range(COEF + 1):
        xdo(f, "wait_send")
        k = f % STEPS
        if f in inputs:
            rdo(f, 0, 1, nx + 1, "wait_send")
        else:
            rdo(f, 0, k + 1, nx + 1 - k, "wait_send")
            for q in range(1, k + 1):
                rdo(f, 2 * q - 1, q, q + 1, "wait_send")
                rdo(f, 2 * q, nx + 1 - q, nx + 2 - q, "wait_send")

    @pl.loop(0, nx)
    def _(i):
        @pl.when(is_end)
        def _():
            end_send(i).wait_send()

        @pl.when(is_mid)
        def _():
            peer_send(i).wait_send()
            back_send(i).wait_send()


def shards(sizes, start_conc, target, log_coef, inv_temp, sched_start):
    inverse_temps = lax.dynamic_slice_in_dim(inv_temp, sched_start[0], STEPS)
    rates = 0.16 * jnp.exp(4.0 * (1.0 - inverse_temps))
    nx, ny, nz = log_coef.shape
    f32 = jnp.float32
    field = pltpu.VMEM((nx, ny, nz), f32)
    dma = pltpu.SemaphoreType.DMA
    fields = COEF + 1
    vmem = pl.BlockSpec(memory_space=pltpu.VMEM)
    hbm = pl.BlockSpec(memory_space=pl.ANY)
    return pl.pallas_call(
        functools.partial(body, sizes),
        out_shape=(
            jax.ShapeDtypeStruct(log_coef.shape, f32),
            jax.ShapeDtypeStruct(start_conc.shape, f32),
            jax.ShapeDtypeStruct(start_conc.shape, f32),
        ),
        in_specs=[pl.BlockSpec(memory_space=pltpu.SMEM), hbm, hbm, hbm],
        out_specs=(vmem, vmem, vmem),
        scratch_shapes=[
            pltpu.VMEM((fields, nx + 2, ny + 16, nz), f32),
            pltpu.VMEM((nx + 1, ny, nz), f32),
            field, field, field, field, field, field, field,
            pltpu.VMEM((nx + 1, ny, nz), f32), pltpu.VMEM((ny + 16, nz), f32),
            dma((3,)), dma((2 * fields,)), dma((2 * fields,)),
            dma((2 * PARTS * fields,)), dma((2 * PARTS * fields,)),
            dma((nx,)), dma((nx,)), dma((nx,)), dma((nx,)),
        ],
        compiler_params=pltpu.CompilerParams(
            collective_id=0, has_side_effects=True, vmem_limit_bytes=60 * 1024 * 1024),
    )(rates, start_conc, target, log_coef)


def solution(mesh):
    placed = (
        P("ens", "gx", "role", None),
        P("ens", "gx", "role", None),
        P("gx", "role", None),
        P(),
        P("ens"),
    )
    return jax.shard_map(
        functools.partial(shards, (mesh.shape["gx"], mesh.shape["role"])),
        mesh=mesh,
        in_specs=placed,
        out_specs=(
            P("gx", "role", None),
            P("ens", "gx", "role", None),
            P("ens", "gx", "role", None),
        ),
        check_vma=False,
    )
```

```python
import functools
import jax
import jax.numpy as jnp
from jax import lax
from jax.experimental import pallas as pl
from jax.experimental.pallas import tpu as pltpu
from jax.sharding import PartitionSpec as P

STEPS = 4
COEF = 2 * STEPS
PARTS = 2 * STEPS - 1
ROWS = 32
FAR = -1e30


def body(
    sizes, rates, start, target, logc, grad_out, adj_out, conc_out,
    F, wx, wyp, wym, wz, D, G, E, M, FX, FY,
    load_sem, xs, xr, rs, rr, sa, sb, re, rm,
):
    ngx, nrole = sizes
    nx, ny, nz = logc.shape
    gx, role, ens = lax.axis_index("gx"), lax.axis_index("role"), lax.axis_index("ens")
    main = pl.ds(8, ny)
    lane = lax.broadcasted_iota(jnp.int32, (ROWS, nz), 1)
    first, last = lane == 0, lane == nz - 1
    chunks = range(8, 8 + ny, ROWS)
    is_end = jnp.logical_or(ens == 0, ens == 3)
    is_mid = jnp.logical_and(ens > 0, ens < 3)
    inputs = {0: start.at[0], STEPS: target.at[0], COEF: logc}
    axes = (("gx", gx, ngx), ("role", role, nrole))
    lower = [index > 0 for _, index, _ in axes]
    upper = [index < count - 1 for _, index, count in axes]

    def has_to(axis, d):
        return upper[axis] if d else lower[axis]

    def has_from(axis, d):
        return lower[axis] if d else upper[axis]

    def xcopy(f, d):
        own = nx if d else 1
        src = inputs[f].at[own - 1] if f in inputs else F.at[f, own, main]
        return pltpu.make_async_remote_copy(
            src, F.at[f, 0 if d else nx + 1, main], xs.at[2 * f + d], xr.at[2 * f + d],
            device_id={"gx": gx + (1 if d else -1)}, device_id_type=pl.DeviceIdType.MESH)

    def rcopy(f, d, part, lo, hi):
        planes = pl.ds(lo, hi - lo)
        row = ny - 8 if d else 0
        if f in inputs:
            src = inputs[f].at[:, pl.ds(row, 8)]
        else:
            src = F.at[f, planes, pl.ds(row + 8, 8)]
        sem = (2 * f + d) * PARTS + part
        return pltpu.make_async_remote_copy(
            src, F.at[f, planes, pl.ds(0 if d else ny + 8, 8)], rs.at[sem], rr.at[sem],
            device_id={"role": role + (1 if d else -1)}, device_id_type=pl.DeviceIdType.MESH)

    def each(axis, make, do):
        for d in (0, 1):
            cond = has_from(axis, d) if do == "wait_recv" else has_to(axis, d)

            @pl.when(cond)
            def _():
                getattr(make(d), do)()

    def xdo(f, do):
        each(0, lambda d: xcopy(f, d), do)

    def rdo(f, part, lo, hi, do):
        each(1, lambda d: rcopy(f, d, part, lo, hi), do)

    barrier = pltpu.get_barrier_semaphore()
    total = jnp.int32(0)
    for name, index, count in axes + (("ens", ens, 4),):
        for cond, to in ((index > 0, -1), (index < count - 1, 1)):
            total = total + cond.astype(jnp.int32)

            @pl.when(cond)
            def _():
                pl.semaphore_signal(barrier, 1, device_id={name: index + to},
                                    device_id_type=pl.DeviceIdType.MESH)
    loads = [
        pltpu.make_async_copy(inputs[f], F.at[f, pl.ds(1, nx), main], load_sem.at[i])
        for i, f in enumerate((COEF, 0, STEPS))
    ]
    for load in loads:
        load.start()
    pl.semaphore_wait(barrier, total)

    for f in (COEF, 0, STEPS):
        rdo(f, 0, 1, nx + 1, "start")
    for f in (COEF, 0, STEPS):
        xdo(f, "start")

    for side in (0, 1):
        @pl.when(jnp.logical_not(upper[0] if side else lower[0]))
        def _():
            @pl.loop(0, COEF)
            def _(f):
                F[f, (nx + 1) * side, main, :] = jnp.zeros((ny, nz), jnp.float32)
            F[COEF, (nx + 1) * side, main, :] = jnp.full((ny, nz), FAR, jnp.float32)

        @pl.when(jnp.logical_not(upper[1] if side else lower[1]))
        def _():
            edge = pl.ds((ny + 8) * side, 8)

            @pl.loop(0, COEF)
            def _(f):
                F[f, pl.ds(1, nx), edge, :] = jnp.zeros((nx, 8, nz), jnp.float32)
            F[COEF, pl.ds(1, nx), edge, :] = jnp.full((nx, 8, nz), FAR, jnp.float32)

    loads[0].wait()
    rdo(COEF, 0, 1, nx + 1, "wait_recv")

    @pl.loop(1, nx + 1)
    def _(p):
        F[COEF, p] = 0.5 * jnp.exp(F[COEF, p])

    def wx_plane(p):
        wx[p] = F[COEF, p, main, :] + F[COEF, p + 1, main, :]

    def diag_plane(p):
        D[p - 1] = D[p - 1] + (wx[p - 1] + wx[p])

    @pl.loop(1, nx + 1)
    def _(p):
        for y in chunks:
            rows = pl.ds(y - 8, ROWS)
            k = F[COEF, p, pl.ds(y, ROWS), :]
            up = k + F[COEF, p, pl.ds(y + 1, ROWS), :]
            down = k + F[COEF, p, pl.ds(y - 1, ROWS), :]
            right = jnp.where(last, 0.0, k + pltpu.roll(k, nz - 1, 1))
            wyp[p - 1, rows, :] = up
            wym[p - 1, rows, :] = down
            wz[p - 1, rows, :] = right
            D[p - 1, rows, :] = (
                up + down + right + pltpu.roll(right, 1, 1)
                + jnp.where(jnp.logical_or(first, last), k, 0.0))

    pl.loop(1, nx)(wx_plane)
    pl.loop(2, nx)(diag_plane)

    def diffuse(k, lo, hi):
        pairs = ((k, rates[k]), (STEPS + k, rates[STEPS - 1 - k]))

        @pl.loop(lo, hi)
        def _(p):
            for y in chunks:
                rows, here = pl.ds(y - 8, ROWS), pl.ds(y, ROWS)
                w0, w1 = wx[p - 1, rows, :], wx[p, rows, :]
                wp, wm = wyp[p - 1, rows, :], wym[p - 1, rows, :]
                wr, diag = wz[p - 1, rows, :], D[p - 1, rows, :]
                for n, (f, rate) in enumerate(pairs):
                    wide = F[f, p, pl.ds(y - 8, ROWS + 16), :]
                    v = wide[8:8 + ROWS]
                    acc = w0 * F[f, p - 1, here, :] + w1 * F[f, p + 1, here, :]
                    acc = acc + wp * wide[9:9 + ROWS]
                    acc = acc + wm * wide[7:7 + ROWS]
                    acc = acc + wr * pltpu.roll(v, nz - 1, 1) + pltpu.roll(wr * v, 1, 1)
                    new = v + rate * (acc - diag * v)
                    if k < STEPS - 1:
                        F[f + 1, p, here, :] = new
                    elif n == 0:
                        conc_out[0, p - 1, rows, :] = new
                    else:
                        adj_out[0, p - 1, rows, :] = new

    def face_x(p):
        for y in chunks:
            here = pl.ds(y, ROWS)
            total_x = 0.0
            for s in range(STEPS):
                cf, af = s, STEPS + (STEPS - 1 - s)
                da = F[af, p, here, :] - F[af, p + 1, here, :]
                dc = F[cf, p, here, :] - F[cf, p + 1, here, :]
                total_x = total_x + rates[s] * (da * dc)
            FX[p, pl.ds(y - 8, ROWS), :] = total_x

    def sens(p):
        edge_y = 0.0
        for s in range(STEPS):
            cf, af = s, STEPS + (STEPS - 1 - s)
            da = F[af, p, pl.ds(0, 8), :] - F[af, p, pl.ds(1, 8), :]
            dc = F[cf, p, pl.ds(0, 8), :] - F[cf, p, pl.ds(1, 8), :]
            edge_y = edge_y + rates[s] * (da * dc)
        FY[pl.ds(0, 8), :] = edge_y
        for y in chunks:
            here, up = pl.ds(y, ROWS), pl.ds(y + 1, ROWS)
            rows = pl.ds(y - 8, ROWS)
            tx, ty, tz, t0 = 0.0, 0.0, 0.0, 0.0
            for s in range(STEPS):
                cf, af = s, STEPS + (STEPS - 1 - s)
                c, a = F[cf, p, here, :], F[af, p, here, :]
                tx = tx + rates[s] * ((a - F[af, p + 1, here, :]) * (c - F[cf, p + 1, here, :]))
                ty = ty + rates[s] * ((a - F[af, p, up, :]) * (c - F[cf, p, up, :]))
                da = a - jnp.where(last, 0.0, pltpu.roll(a, nz - 1, 1))
                dc = c - jnp.where(last, 0.0, pltpu.roll(c, nz - 1, 1))
                tz = tz + rates[s] * (da * dc)
                t0 = t0 + rates[s] * (a[:, :128] * c[:, :128])
            FX[p, rows, :] = tx
            FY[here, :] = ty
            low_z = jnp.where(first, jnp.concatenate([t0] * (nz // 128), axis=1), pltpu.roll(tz, 1, 1))
            low_y = FY[pl.ds(y - 1, ROWS), :]
            G[p - 1, rows, :] = -0.5 * ((tx + FX[p - 1, rows, :]) + (ty + low_y) + (tz + low_z))

    def ens_copy(src, dst, send, recv, to):
        return pltpu.make_async_remote_copy(
            src, dst, send, recv, device_id={"ens": to}, device_id_type=pl.DeviceIdType.MESH)

    quarter, half = STEPS, nx - 2 * STEPS

    def plane(i):
        outside, side, ring = lax.div(i, half), lax.rem(i, 2), lax.div(i, 2) - half // 2
        pair = quarter - 1 - ring + side * (half + 1 + 2 * ring)
        return (1 - outside) * (i + quarter) + outside * pair

    def end_send(i):
        q = plane(i)
        return ens_copy(G.at[q], E.at[q], sa.at[i], re.at[i], 1 + ens // 3)

    def peer_send(i):
        q = plane(i)
        return ens_copy(E.at[q], M.at[q], sa.at[i], rm.at[i], 3 - ens)

    def back_send(i):
        q = plane(i)
        return ens_copy(G.at[q], M.at[q], sb.at[i], rm.at[i], (ens - 1) * 3)

    def gradient(lo, hi):
        @pl.loop(lo, hi)
        def _(i):
            sens(plane(i) + 1)

            @pl.when(is_end)
            def _():
                end_send(i).start()

    def merge_one(i):
        q = plane(i)
        end_send(i).wait_recv()
        E[q] = E[q] + G[q]
        peer_send(i).start()

    def close_one(i):
        q = plane(i)
        peer_send(i).wait_recv()
        G[q] = E[q] + M[q]
        back_send(i).start()
        grad_out[q] = 2.0 * F[COEF, q + 1, main, :] * G[q]

    def merge(lo, hi):
        @pl.when(is_mid)
        def _():
            pl.loop(lo, hi)(merge_one)

    def close(lo, hi):
        @pl.when(is_mid)
        def _():
            pl.loop(lo, hi)(close_one)

    def finish(lo, hi):
        @pl.when(is_end)
        def _():
            @pl.loop(lo, hi)
            def _(i):
                q = plane(i)
                back_send(i).wait_recv()
                grad_out[q] = 2.0 * F[COEF, q + 1, main, :] * M[q]

    loads[1].wait()
    loads[2].wait()
    for f in (0, STEPS):
        rdo(f, 0, 1, nx + 1, "wait_recv")
    def inner(k):
        lo, hi = k + 2, nx - k
        if k > 0:
            for f in (k, STEPS + k):
                rdo(f, 0, lo - 1, hi + 1, "wait_recv")
        diffuse(k, lo, hi)
        for f in (k + 1, STEPS + k + 1):
            rdo(f, 0, lo, hi, "start")

    def single(level, q, do):
        for f in (level, STEPS + level):
            rdo(f, 2 * q - 1, q, q + 1, do)
            rdo(f, 2 * q, nx + 1 - q, nx + 2 - q, do)

    def arrive(k):
        for f in (k, STEPS + k):
            xdo(f, "wait_recv")
        for level in range(max(k, 1), STEPS):
            if k > 0:
                single(level, level - k + 1, "wait_recv")

    def wave(k, j):
        q = j - k + 1
        diffuse(j, q, q + 1)
        diffuse(j, nx + 1 - q, nx + 2 - q)
        if j == k:
            for f in (k + 1, STEPS + k + 1):
                xdo(f, "start")
        single(j + 1, q, "start")

    def ring(k):
        face_x(quarter - k - 1)
        gradient(half + 2 * k, half + 2 * k + 2)

    inner(0)
    xdo(COEF, "wait_recv")
    for p in (0, nx + 1):
        F[COEF, p, main, :] = 0.5 * jnp.exp(F[COEF, p, main, :])
    wx_plane(0)
    wx_plane(nx)
    diag_plane(1)
    diag_plane(nx)
    inner(1)
    arrive(0)
    wave(0, 0)
    inner(2)
    for f in (STEPS - 1, COEF - 1):
        rdo(f, 0, STEPS, nx - STEPS + 2, "wait_recv")
    face_x(quarter)
    gradient(0, half)
    merge(0, 1)
    wave(0, 1)
    merge(1, 2)
    wave(0, 2)
    ring(0)
    merge(2, 3)
    arrive(1)
    wave(1, 1)
    merge(3, 4)
    close(0, 1)
    wave(1, 2)
    ring(1)
    merge(4, 5)
    close(1, 2)
    diffuse(STEPS - 1, quarter + 1, half + 1)
    merge(5, 6)
    close(2, 3)
    arrive(2)
    wave(2, 2)
    ring(2)
    merge(6, 7)
    close(3, 5)
    diffuse(STEPS - 1, half + 1, nx - quarter + 1)
    merge(7, half)
    close(5, 6)
    arrive(3)
    ring(3)
    merge(half, half + 1)
    close(6, 7)
    diffuse(STEPS - 1, 1, quarter + 1)
    merge(half + 1, half + 2)
    close(7, half)
    diffuse(STEPS - 1, nx - quarter + 1, nx + 1)

    @pl.when(is_mid)
    def _():
        @pl.loop(half + 2, nx)
        def _(i):
            merge_one(i)
            close_one(i - 2)
    close(nx - 2, nx)
    finish(0, nx)

    for f in range(COEF + 1):
        xdo(f, "wait_send")
        k = f % STEPS
        if f in inputs:
            rdo(f, 0, 1, nx + 1, "wait_send")
        else:
            rdo(f, 0, k + 1, nx + 1 - k, "wait_send")
            for q in range(1, k + 1):
                rdo(f, 2 * q - 1, q, q + 1, "wait_send")
                rdo(f, 2 * q, nx + 1 - q, nx + 2 - q, "wait_send")

    @pl.loop(0, nx)
    def _(i):
        @pl.when(is_end)
        def _():
            end_send(i).wait_send()

        @pl.when(is_mid)
        def _():
            peer_send(i).wait_send()
            back_send(i).wait_send()


def shards(sizes, start_conc, target, log_coef, inv_temp, sched_start):
    inverse_temps = lax.dynamic_slice_in_dim(inv_temp, sched_start[0], STEPS)
    rates = 0.16 * jnp.exp(4.0 * (1.0 - inverse_temps))
    nx, ny, nz = log_coef.shape
    f32 = jnp.float32
    field = pltpu.VMEM((nx, ny, nz), f32)
    dma = pltpu.SemaphoreType.DMA
    fields = COEF + 1
    vmem = pl.BlockSpec(memory_space=pltpu.VMEM)
    hbm = pl.BlockSpec(memory_space=pl.ANY)
    return pl.pallas_call(
        functools.partial(body, sizes),
        out_shape=(
            jax.ShapeDtypeStruct(log_coef.shape, f32),
            jax.ShapeDtypeStruct(start_conc.shape, f32),
            jax.ShapeDtypeStruct(start_conc.shape, f32),
        ),
        in_specs=[pl.BlockSpec(memory_space=pltpu.SMEM), hbm, hbm, hbm],
        out_specs=(vmem, vmem, vmem),
        scratch_shapes=[
            pltpu.VMEM((fields, nx + 2, ny + 16, nz), f32),
            pltpu.VMEM((nx + 1, ny, nz), f32),
            field, field, field, field, field, field, field,
            pltpu.VMEM((nx + 1, ny, nz), f32), pltpu.VMEM((ny + 16, nz), f32),
            dma((3,)), dma((2 * fields,)), dma((2 * fields,)),
            dma((2 * PARTS * fields,)), dma((2 * PARTS * fields,)),
            dma((nx,)), dma((nx,)), dma((nx,)), dma((nx,)),
        ],
        compiler_params=pltpu.CompilerParams(
            collective_id=0, has_side_effects=True, vmem_limit_bytes=60 * 1024 * 1024),
    )(rates, start_conc, target, log_coef)


def solution(mesh):
    placed = (
        P("ens", "gx", "role", None),
        P("ens", "gx", "role", None),
        P("gx", "role", None),
        P(),
        P("ens"),
    )
    return jax.shard_map(
        functools.partial(shards, (mesh.shape["gx"], mesh.shape["role"])),
        mesh=mesh,
        in_specs=placed,
        out_specs=(
            P("gx", "role", None),
            P("ens", "gx", "role", None),
            P("ens", "gx", "role", None),
        ),
        check_vma=False,
    )
```
